256 devices in a mesh: rep: 16 (over z_hi, x, core), tp: 16 (over y, z_lo).
Axes of the slice: x: 4, y: 4, z: 8 (z_hi: 2, z_lo: 4; z = z_hi * 4 + z_lo), core: 2. Of those that a mesh axis runs over, the one named last changes fastest.
Arguments:
- tokens: bfloat16 [16384, 2048], P('rep', 'tp'), may hold values from -6 to 6
- doc_starts: int32 [16, 32], P('rep'), may hold values from 0 to 1023, as said below
- owner_map: int32 [16], replicated, may hold values from 0 to 15, as said below
- in_weight: bfloat16 [16, 2, 2048, 12288], P('rep', None, None, 'tp'), may hold values from -0.125 to 0.125
- rate_weight: bfloat16 [16, 2, 2048, 64], P('rep', None, None, 'tp'), may hold values from -0.125 to 0.125
- out_weight: bfloat16 [16, 2, 4096, 2048], P('rep', None, None, 'tp'), may hold values from -0.09375 to 0.09375
- decay_log: bfloat16 [16, 2, 32], P('rep', None, 'tp'), may hold values from -3 to 1
- decay_bias: bfloat16 [16, 2, 32], P('rep', None, 'tp'), may hold values from -4 to 1
- norm_gain: bfloat16 [16, 2, 2048], P('rep', None, 'tp'), may hold values from 0.5 to 1.5
- head_gain: bfloat16 [16, 2, 128], P('rep'), may hold values from 0.5 to 1.5
Outputs:
- prefill_out: bfloat16 [16384, 2048], P('rep', 'tp')
The draws below stay inside these ranges and needn't reach their ends.
Inputs may be any that keep to these rules, and one draw needn't show every extreme that they name: `owner_map`: entry j names the replica whose copy of tensor block j is current; the first and the last replica both occur. `doc_starts`: each row rises strictly, begins with 0 and ends with 1023.
All inputs are finite; a program needn't handle non-finite values.
Results may differ from the reference program's by a relative error of at most 0.023.
Values may be sent and summed in bfloat16 or wider, within the bound.
No kernel may reach another device: no remote copies, remote signals or barrier semaphores. Data moves between devices by JAX's collectives and lax.ppermute only.
A program may use at most 128 MiB of HBM per device.

```python
import math
import jax
import jax.numpy as jnp
from jax import lax

D = 2048
DK = 128
DV = 128
KH_DEV = 1
VH_DEV = 2
KEY_HEADS = 16
VAL_HEADS = 32
PROJ_DEV = 768
PROJ = 12288
LAYERS = 2
TOK = 1024
DOCS = 32
TOKENS = 16384
N_REP = 16
N_TP = 16


def draw_owner_map(key, part):
    key = jax.random.fold_in(key, 7)
    first, second = jax.random.split(key)
    chosen = jax.random.randint(first, (N_TP,), 0, N_REP)
    places = jax.random.permutation(second, N_TP)
    chosen = chosen.at[places[0]].set(N_REP - 1)
    chosen = chosen.at[places[1]].set(0)
    return chosen.astype(jnp.int32)


def draw_doc_starts(key, part):
    key = jax.random.fold_in(key, 13)
    row_keys = jax.random.split(key, N_REP)

    def one_row(row_key):
        inner_starts = jax.random.permutation(row_key, TOK - 2)[:DOCS - 2] + 1
        fixed_ends = jnp.array([0, TOK - 1], jnp.int32)
        return jnp.sort(jnp.concatenate([fixed_ends, inner_starts.astype(jnp.int32)]))
    return jax.vmap(one_row)(row_keys).astype(jnp.int32)


def block_levels(key, dims, cuts, smallest, largest):
    def one(dim, parts):
        draws = jax.random.uniform(jax.random.fold_in(jax.random.fold_in(key, 6), dim), (parts,), jnp.float32, smallest / len(cuts), largest / len(cuts))
        return jnp.repeat(jnp.exp(draws), dims[dim] // parts).reshape((-1,) + (1,) * (len(dims) - dim - 1))

    level = one(*cuts[0])
    for cut in cuts[1:]:
        level = level * one(*cut)
    return level


def gaussian(key, shape, scale, most, cuts=(), kind=jnp.bfloat16):
    entries = jax.random.normal(key, shape, jnp.float32) * scale
    if len(cuts) > 0:
        entries = block_levels(key, shape, cuts, -0.22, 0.18) * entries
    return jnp.clip(entries, min=-most, max=most).astype(kind)


def setup_inputs(seed: int = 0) -> dict:
    streams_of = jax.random.split(jax.random.key(seed), 11)
    tokens = gaussian(streams_of[0], (TOKENS, D), 1.0, 6.0, ((0, 16), (1, 16)))
    doc_starts = draw_doc_starts(jax.random.fold_in(streams_of[10], 71), 0)
    owner_map = draw_owner_map(jax.random.fold_in(streams_of[10], 71), 0)
    in_weight = gaussian(streams_of[3], (N_REP, LAYERS, D, PROJ), D ** -0.5, 0.125, ((0, 16), (3, 16)))
    rate_weight = gaussian(streams_of[4], (N_REP, LAYERS, D, 2 * VAL_HEADS), D ** -0.5, 0.125, ((0, 16), (3, 16)))
    out_weight = gaussian(streams_of[5], (N_REP, LAYERS, VAL_HEADS * DV, D), (VAL_HEADS * DV) ** -0.5, 0.09375, ((0, 16), (3, 16)))
    decay_log = jnp.clip(-3.0 + 4.0 * jax.random.uniform(streams_of[6], (N_REP, LAYERS, VAL_HEADS), jnp.float32) ** block_levels(streams_of[6], (N_REP, LAYERS, VAL_HEADS), ((0, 16), (2, 16)), -0.2, 0.2), -3.0, 1.0).astype(jnp.bfloat16)
    decay_bias = jnp.clip(-4.0 + 5.0 * jax.random.uniform(streams_of[7], (N_REP, LAYERS, VAL_HEADS), jnp.float32) ** block_levels(streams_of[7], (N_REP, LAYERS, VAL_HEADS), ((0, 16), (2, 16)), -0.2, 0.2), -4.0, 1.0).astype(jnp.bfloat16)
    norm_gain = jnp.clip(1.0 + 0.1 * jax.random.normal(streams_of[8], (N_REP, LAYERS, D), jnp.float32), 0.5, 1.5).astype(jnp.bfloat16)
    head_gain = jnp.clip(1.0 + 0.1 * jax.random.normal(streams_of[9], (N_REP, LAYERS, DV), jnp.float32), 0.5, 1.5).astype(jnp.bfloat16)
    return dict(tokens=tokens, doc_starts=doc_starts, owner_map=owner_map, in_weight=in_weight, rate_weight=rate_weight, out_weight=out_weight, decay_log=decay_log, decay_bias=decay_bias, norm_gain=norm_gain, head_gain=head_gain)


epsilon = 1e-06
highest = lax.Precision.HIGHEST

def delta_spans(queries, key_rows, values, write_rate, decays, doc_ids):
    seq_len, head_count, key_dim = key_rows.shape
    value_dim = values.shape[-1]
    block_len = min(64, seq_len)
    block_count = seq_len // block_len
    positions = jnp.arange(block_len, dtype=jnp.int32)
    strict = (positions[:, None] > positions[None, :]).astype(jnp.float32)
    inclusive = (positions[:, None] >= positions[None, :]).astype(jnp.float32)
    identity_mat = jnp.eye(block_len, dtype=jnp.float32)

    def blocked(array):
        return array.reshape((block_count, block_len) + array.shape[1:])

    def advance(carry, inputs):
        memory, last_doc = carry
        block_query, block_key, block_value, block_rate, block_decay, block_ids = inputs
        cumulative = jnp.cumsum(block_decay, axis=0)
        same_doc = (block_ids[:, None] == block_ids[None, :]).astype(jnp.float32)
        spread = cumulative[:, None, :] - cumulative[None, :, :]
        pair_decay = jnp.exp(jnp.minimum(spread, 0.0)) * same_doc[:, :, None]
        pair_decay = jnp.transpose(pair_decay, (2, 0, 1))
        carried = jnp.exp(cumulative) * (block_ids == last_doc).astype(jnp.float32)[:, None]
        key_gram = jnp.einsum('ihd,jhd->hij', block_key, block_key, precision=highest)
        lower = jnp.transpose(block_rate)[:, :, None] * key_gram * pair_decay * strict
        from_memory = jnp.einsum('ihd,hde->ihe', block_key, memory, precision=highest)
        target = block_rate[:, :, None] * (block_value - carried[:, :, None] * from_memory)
        target = jnp.transpose(target, (1, 0, 2))
        updates = jax.scipy.linalg.solve_triangular(lower + identity_mat, target, lower=True, unit_diagonal=True)
        scores = jnp.einsum('ihd,jhd->hij', block_query, block_key, precision=highest) * pair_decay * inclusive
        output = carried[:, :, None] * jnp.einsum('ihd,hde->ihe', block_query, memory, precision=highest)
        output = output + jnp.einsum('hij,hje->ihe', scores, updates, precision=highest)
        tail = pair_decay[:, -1, :]
        memory_next = carried[-1][:, None, None] * memory + jnp.einsum('jhd,hj,hje->hde', block_key, tail, updates, precision=highest)
        return ((memory_next, block_ids[-1]), output)
    start_memory = jnp.zeros((head_count, key_dim, value_dim), jnp.float32)
    start_doc = jnp.zeros((), jnp.int32)
    inputs = (blocked(queries), blocked(key_rows), blocked(values), blocked(write_rate), blocked(decays), blocked(doc_ids))
    carry_out, outputs = lax.scan(advance, (start_memory, start_doc), inputs)
    return outputs.reshape(seq_len, head_count, value_dim)

def head_outputs(queries, key_rows, values, gate_rows, rate_raw, decay_raw, decay_log, decay_bias, head_gain, doc_ids):
    repeat_count = values.shape[1] // queries.shape[1]
    query_wide = queries.astype(jnp.float32)
    key_wide = key_rows.astype(jnp.float32)
    unit_query = query_wide * lax.rsqrt(lax.optimization_barrier(jnp.sum(query_wide * query_wide, axis=-1, keepdims=True)) + epsilon) / math.sqrt(queries.shape[-1])
    unit_key = key_wide * lax.rsqrt(lax.optimization_barrier(jnp.sum(key_wide * key_wide, axis=-1, keepdims=True)) + epsilon)
    unit_query = jnp.repeat(unit_query, repeat_count, axis=1)
    unit_key = jnp.repeat(unit_key, repeat_count, axis=1)
    write_rate = jax.nn.sigmoid(rate_raw)
    decays = -jnp.exp(decay_log.astype(jnp.float32)) * jax.nn.softplus(decay_raw + decay_bias.astype(jnp.float32))
    mixed = delta_spans(unit_query, unit_key, values.astype(jnp.float32), write_rate, decays, doc_ids)
    scaled = mixed * lax.rsqrt(lax.optimization_barrier(jnp.mean(mixed * mixed, axis=-1, keepdims=True)) + epsilon)
    scaled = scaled * head_gain.astype(jnp.float32) * jax.nn.silu(gate_rows.astype(jnp.float32))
    return scaled.astype(jnp.bfloat16).reshape(values.shape[0], -1)

def select_blocks(stacked, owner_map):
    replicas, layer_count, inner_dim, col_total = stacked.shape
    shard_count = owner_map.shape[0]
    blocks = stacked.reshape(replicas, layer_count, inner_dim, shard_count, col_total // shard_count)
    picked = blocks[owner_map, :, :, jnp.arange(shard_count, dtype=jnp.int32), :]
    return jnp.transpose(picked, (1, 2, 0, 3)).reshape(layer_count, inner_dim, col_total)

def block_products(head_out, out_w):
    block_width = VH_DEV * DV
    head_blocks = head_out.reshape(TOK, N_TP, block_width)
    weight_blocks = out_w.reshape(N_TP, block_width, D)

    def one_block(total, index):
        part = jnp.dot(head_blocks[:, index, :].astype(jnp.float32), weight_blocks[index].astype(jnp.float32), preferred_element_type=jnp.float32)
        rounded = lax.optimization_barrier(part.astype(jnp.bfloat16))
        return (total + rounded.astype(jnp.float32), None)
    total, unused = lax.scan(one_block, jnp.zeros((TOK, D), jnp.float32), jnp.arange(N_TP, dtype=jnp.int32))
    return total

def group_pass(block_tokens, start_row, in_w, rate_w, out_w, decay_log, decay_bias, norm_gain, head_gain):
    stream_wide = block_tokens.astype(jnp.float32)
    normed = stream_wide * lax.rsqrt(lax.optimization_barrier(jnp.mean(stream_wide * stream_wide, axis=-1, keepdims=True)) + epsilon)
    normed = (normed * norm_gain.astype(jnp.float32)).astype(jnp.bfloat16)
    projected = jnp.dot(normed.astype(jnp.float32), in_w.astype(jnp.float32), preferred_element_type=jnp.float32).astype(jnp.bfloat16)
    projected = projected.reshape(TOK, N_TP, PROJ_DEV)
    key_width = KH_DEV * DK
    value_width = VH_DEV * DV
    queries = projected[:, :, :key_width].reshape(TOK, KEY_HEADS, DK)
    key_rows = projected[:, :, key_width:2 * key_width].reshape(TOK, KEY_HEADS, DK)
    values = projected[:, :, 2 * key_width:2 * key_width + value_width].reshape(TOK, VAL_HEADS, DV)
    gate_rows = projected[:, :, 2 * key_width + value_width:].reshape(TOK, VAL_HEADS, DV)
    rates = jnp.dot(normed.astype(jnp.float32), rate_w.astype(jnp.float32), preferred_element_type=jnp.float32).reshape(TOK, N_TP, 2, VH_DEV)
    rate_raw = rates[:, :, 0].reshape(TOK, VAL_HEADS)
    decay_raw = rates[:, :, 1].reshape(TOK, VAL_HEADS)
    token_pos = jnp.arange(TOK, dtype=jnp.int32)
    doc_ids = lax.optimization_barrier(jnp.sum((start_row[None, :] <= token_pos[:, None]).astype(jnp.int32), axis=1)).astype(jnp.int32)
    head_out = head_outputs(queries, key_rows, values, gate_rows, rate_raw, decay_raw, decay_log, decay_bias, head_gain, doc_ids)
    blended = block_products(head_out, out_w) + stream_wide
    return blended.astype(jnp.bfloat16)

def reference(tokens, doc_starts, owner_map, in_weight, rate_weight, out_weight, decay_log, decay_bias, norm_gain, head_gain):
    chosen_in = select_blocks(in_weight, owner_map)
    chosen_rate = select_blocks(rate_weight, owner_map)
    chosen_out = select_blocks(out_weight, owner_map)
    chosen_log = select_blocks(decay_log[:, :, None, :], owner_map)[:, 0]
    chosen_bias = select_blocks(decay_bias[:, :, None, :], owner_map)[:, 0]
    chosen_norm = select_blocks(norm_gain[:, :, None, :], owner_map)[:, 0]
    picked_gain = jnp.repeat(head_gain[owner_map], VH_DEV, axis=0)
    chosen_head = jnp.transpose(picked_gain, (1, 0, 2))
    stream = tokens.reshape(N_REP, TOK, D)
    for layer_no in range(LAYERS):

        def one_group(pair, layer_no=layer_no):
            return group_pass(pair[0], pair[1], chosen_in[layer_no], chosen_rate[layer_no], chosen_out[layer_no], chosen_log[layer_no], chosen_bias[layer_no], chosen_norm[layer_no], chosen_head[layer_no])
        stream = lax.map(one_group, (stream, doc_starts))
    return stream.reshape(TOKENS, D)
```

```python
import functools
import math

import jax
import jax.numpy as jnp
from jax import lax
from jax.experimental import pallas as pl
from jax.experimental.pallas import tpu as pltpu
from jax.sharding import PartitionSpec as P

D = 2048
DK = 128
DV = 128
VH_DEV = 2
PROJ_DEV = 768
TOK = 1024
CHUNK = 128
HALF = TOK // 2
CHUNKS = HALF // CHUNK
GROUP = 4
epsilon = 1e-06

f32 = jnp.float32
bf16 = jnp.bfloat16


def rep_perm(z_shift, x_shift, core_shift):
    pairs = []
    for i in range(16):
        zh, x, c = i // 8, (i // 2) % 4, i % 2
        pairs.append((i, ((zh + z_shift) % 2) * 8 + ((x + x_shift) % 4) * 2 + (c + core_shift) % 2))
    return pairs


def tp_perm(y_shift, z_flip):
    return [(i, ((i // 4 + y_shift) % 4) * 4 + ((i % 4) ^ z_flip)) for i in range(16)]


def pick(array, index, axis=0):
    return lax.dynamic_index_in_dim(array, index, axis, keepdims=False)


def no_work(*refs):
    pass


def fence(values, others):
    anywhere = pl.BlockSpec(memory_space=pl.ANY)
    return pl.pallas_call(
        no_work,
        out_shape=[jax.ShapeDtypeStruct(v.shape, v.dtype) for v in values],
        in_specs=[anywhere] * (len(values) + len(others)),
        out_specs=[anywhere] * len(values),
        input_output_aliases={n: n for n in range(len(values))},
    )(*values, *others)


def to_x(array, d):
    return lax.ppermute(array, "rep", rep_perm(0, d, 0))


def to_y(array, t):
    return lax.ppermute(array, "tp", tp_perm(t, 0))


def to_z(array, s):
    return lax.ppermute(array, "tp", tp_perm(0, s))


def other_plane(array):
    return lax.ppermute(array, "rep", rep_perm(1, 0, 0))


def other_core(array):
    return lax.ppermute(array, "rep", rep_perm(0, 0, 1))


def scatter(half, x, owner_x):
    moved = [to_x(pick(half, (x + d) % 4), d) for d in (1, 2, 3)]
    delta = (x - owner_x) % 4
    current = pick(half, x)
    for d in (1, 2, 3):
        current = jnp.where(delta == d, moved[d - 1], current)
    return current


def over_y(array):
    return [array] + [to_y(array, t) for t in (1, 2, 3)]


def over_z(block):
    return jnp.stack([block] + [to_z(block, s) for s in (1, 2, 3)])


def sum_y(slabs, block):
    came = [slabs[0]] + [to_y(slabs[t], t) for t in (1, 2, 3)]
    total = sum(part[0].astype(f32) for part in came) + block.astype(f32)
    return total, [sum(part[s].astype(f32) for part in came).astype(bf16) for s in (1, 2, 3)]


def sum_z(total, rows):
    for s in (1, 2, 3):
        total = total + to_z(rows[s - 1], s).astype(f32)
    return total.astype(bf16)


def dot(a, b):
    return jnp.dot(a.astype(bf16), b.astype(bf16), preferred_element_type=f32)


def dot_nt(a, b):
    return lax.dot_general(
        a.astype(bf16), b.astype(bf16), (((1,), (1,)), ((), ())), preferred_element_type=f32
    )


def kernel(layer_no, part, place, doc_row, doc_col, gains, before, *refs):
    by_y, in_pieces, heads, memory_out = refs[0:4], refs[4:-13], refs[-13], refs[-12]
    normed, in_w, rate_w, proj, rates, kw, kb, qt, o1, keep, mems = refs[-11:]
    skipped = 0 if layer_no else part * HALF

    rate_w[...] = jnp.zeros_like(rate_w)
    for d in range(4):
        for e in range(2):
            if layer_no:
                p = 2 * d + e
                piece = in_pieces[0].at[p]
            else:
                p = place[16 + 2 * d + e]
                piece = in_pieces[2 * e + 1].at[0] if d == 2 else in_pieces[2 * e].at[(0, 1, None, 2)[d]]
            in_w[pl.ds(pl.multiple_of(p * 256, 256), 256), :] = piece[0:256, :]
            rate_w[0:16, pl.ds(pl.multiple_of(p * 256, 256), 256)] = piece[256:272, 0:256]
    extra = in_pieces[0][0, 256:272, 0:128].astype(f32)
    head_gain = extra[4:5, :]
    log_row = extra[5:6, :]
    bias_row = extra[6:7, :]

    def norm_rows(r, _):
        rows = pl.ds(pl.multiple_of(skipped + r * 128, 128), 128)
        place_rows = pl.ds(pl.multiple_of(r * 128, 128), 128)
        squares = jnp.zeros((128, 128), f32)
        for n in range(16):
            wide = by_y[n // 4][n % 4, rows, :].astype(f32)
            squares = squares + wide * wide
        scale = lax.rsqrt(jnp.sum(squares, axis=1, keepdims=True) / D + epsilon)
        for n in range(16):
            b = place[n]
            gain = gains[layer_no, b].astype(f32)[0:1, :]
            wide = by_y[n // 4][n % 4, rows, :].astype(f32) * scale * gain
            normed[place_rows, pl.ds(pl.multiple_of(b * 128, 128), 128)] = wide.astype(bf16)
        return 0

    lax.fori_loop(0, HALF // 128, norm_rows, 0)

    def project(r, _):
        rows = pl.ds(pl.multiple_of(r * 256, 256), 256)
        left = normed[rows, :]
        proj[rows, :] = jnp.dot(left, in_w[...], preferred_element_type=f32).astype(bf16)
        rates[rows, :] = dot_nt(left, rate_w[...])
        return 0

    lax.fori_loop(0, HALF // 256, project, 0)

    ii = lax.broadcasted_iota(jnp.int32, (CHUNK, CHUNK), 0)
    jj = lax.broadcasted_iota(jnp.int32, (CHUNK, CHUNK), 1)
    eye = (ii == jj).astype(f32)
    inclusive = ii >= jj

    def prepare(group, _):
        lowers, solved, scores, rights, tails, lasts, queries, carries = [], [], [], [], [], [], [], []
        for n in range(GROUP):
            c = group * GROUP + n
            rows = pl.ds(pl.multiple_of(c * CHUNK, CHUNK), CHUNK)
            query = proj[rows, 0:128].astype(f32)
            key = proj[rows, 128:256].astype(f32)
            query = query * (
                lax.rsqrt(jnp.sum(query * query, axis=1, keepdims=True) + epsilon) / math.sqrt(DK)
            )
            key = key * lax.rsqrt(jnp.sum(key * key, axis=1, keepdims=True) + epsilon)
            key_gram = dot_nt(key, key)
            query_gram = dot_nt(query, key)
            raw = rates[rows, :]
            beta = 1.0 / (1.0 + jnp.exp(-raw))
            moved = raw + bias_row
            soft = jnp.maximum(moved, 0.0) + jnp.log1p(jnp.exp(-jnp.abs(moved)))
            decay = -jnp.exp(log_row) * soft
            cumulative = jnp.dot(
                inclusive.astype(f32), decay, preferred_element_type=f32, precision=lax.Precision.HIGHEST
            )
            across = cumulative.T
            docs = doc_col[pl.ds(pl.multiple_of(part * HALF + c * CHUNK, CHUNK), CHUNK), :]
            same = docs[:, 0:1] == doc_row[pl.ds(part * CHUNKS + c, 1), :]
            kept = jnp.logical_and(same, inclusive)
            for h in range(VH_DEV):
                cum = cumulative[:, 2 + h : 3 + h]
                pair = jnp.where(
                    kept, jnp.exp(jnp.minimum(cum - across[2 + h : 3 + h, :], 0.0)), 0.0
                )
                carried = jnp.exp(cum) * docs[:, 1:2]
                rate = beta[:, h : h + 1]
                tail = jnp.exp(jnp.minimum(cum[CHUNK - 1 :, :] - cum, 0.0)) * docs[:, 2:3]
                lower = jnp.where(ii > jj, rate * key_gram * pair, 0.0)
                lowers.append(lower.astype(bf16))
                solved.append(eye - jnp.where(ii // 2 == jj // 2, lower, 0.0))
                scores.append((query_gram * pair).astype(bf16))
                value = proj[rows, 256 + h * 128 : 384 + h * 128].astype(f32)
                rights.append(
                    jnp.concatenate(
                        [(rate * value).astype(bf16), (rate * carried * key).astype(bf16)], axis=1
                    )
                )
                tails.append((key * tail).T.astype(bf16))
                lasts.append(carried[CHUNK - 1 :, :])
                queries.append(carried * query)
        size = 2
        while size < CHUNK:
            corner = jnp.logical_and(
                ii // (2 * size) == jj // (2 * size),
                jnp.logical_and((ii // size) % 2 == 1, (jj // size) % 2 == 0),
            )
            halves = []
            for n in range(len(lowers)):
                halves.append(dot(jnp.where(corner, lowers[n], jnp.zeros_like(lowers[n])), solved[n]))
            for n in range(len(lowers)):
                solved[n] = solved[n] - dot(solved[n], halves[n])
            size *= 2
        updates = [dot(solved[n], rights[n]).astype(bf16) for n in range(len(lowers))]
        for n in range(len(lowers)):
            m = group * GROUP * VH_DEV + n
            through = dot(scores[n], updates[n])
            o1[m] = through[:, 0:128]
            qt[m] = (queries[n] - through[:, 128:256]).astype(bf16)
            stored = dot(tails[n], updates[n])
            kb[m] = stored[:, 0:128]
            kw[m] = stored[:, 128:256].astype(bf16)
            keep[m] = jnp.broadcast_to(lasts[n], (8, 128))
        return 0

    lax.fori_loop(0, CHUNKS // GROUP, prepare, 0)

    memory = [before[h] for h in range(VH_DEV)]
    for c in range(CHUNKS):
        for h in range(VH_DEV):
            m = c * VH_DEV + h
            narrow = memory[h].astype(bf16)
            mems[m] = narrow
            if c < CHUNKS - 1 or part == 0:
                memory[h] = keep[m][0:1, :] * memory[h] + (kb[m] - dot(kw[m], narrow))

    for h in range(VH_DEV):
        memory_out[h] = memory[h]

    def finish(c, _):
        rows = pl.ds(pl.multiple_of(c * CHUNK, CHUNK), CHUNK)
        for h in range(VH_DEV):
            m = c * VH_DEV + h
            mixed = o1[m] + dot(qt[m], mems[m])
            scaled = mixed * lax.rsqrt(jnp.mean(mixed * mixed, axis=1, keepdims=True) + epsilon)
            gate = proj[rows, 512 + h * 128 : 640 + h * 128].astype(f32)
            scaled = scaled * head_gain * (gate / (1.0 + jnp.exp(-gate)))
            heads[rows, h * 128 : (h + 1) * 128] = scaled.astype(bf16)
        return 0

    lax.fori_loop(0, CHUNKS, finish, 0)


def out_kernel(layer_no, place, heads, held, sibling, *refs):
    slabs, out_w = refs[0:4], refs[4]
    y, z = place[24], place[25]
    for d in range(4):
        for e in range(2):
            rows = pl.ds(pl.multiple_of(place[16 + 2 * d + e] * 32, 32), 32)
            for c in range(16):
                columns = pl.ds(pl.multiple_of(((c % 4) ^ z) * 128, 128), 128)
                out_w[(c // 4 + 4 - y) % 4, rows, columns] = (held, sibling)[e][d, layer_no, c]

    def outputs(r, _):
        rows = pl.ds(pl.multiple_of(r * 256, 256), 256)
        left = heads[rows, :]
        for t in range(4):
            made = jnp.dot(left, out_w[t], preferred_element_type=f32).astype(bf16)
            for s in range(4):
                slabs[t][s, rows, :] = made[:, s * 128 : (s + 1) * 128]
        return 0

    lax.fori_loop(0, HALF // 256, outputs, 0)


VMEM = pl.BlockSpec(memory_space=pltpu.VMEM)
SMEM = pl.BlockSpec(memory_space=pltpu.SMEM)
PARAMS = pltpu.CompilerParams(vmem_limit_bytes=56 * 1024 * 1024)


def heads_call(layer_no, part, place, doc_row, doc_col, gains, before, by_y, in_pieces):
    return pl.pallas_call(
        functools.partial(kernel, layer_no, part),
        out_shape=[
            jax.ShapeDtypeStruct((HALF, 256), bf16),
            jax.ShapeDtypeStruct((VH_DEV, DK, DV), f32),
        ],
        in_specs=[SMEM] + [VMEM] * (4 + len(by_y) + len(in_pieces)),
        out_specs=[VMEM] * 2,
        scratch_shapes=[
            pltpu.VMEM((HALF, D), bf16),
            pltpu.VMEM((D, PROJ_DEV), bf16),
            pltpu.VMEM((128, D), bf16),
            pltpu.VMEM((HALF, PROJ_DEV), bf16),
            pltpu.VMEM((HALF, 128), f32),
            pltpu.VMEM((8, 128, 128), bf16),
            pltpu.VMEM((8, 128, 128), f32),
            pltpu.VMEM((8, 128, 128), bf16),
            pltpu.VMEM((8, 128, 128), f32),
            pltpu.VMEM((8, 8, 128), f32),
            pltpu.VMEM((8, 128, 128), bf16),
        ],
        compiler_params=PARAMS,
        cost_estimate=pl.CostEstimate(
            flops=4 * TOK * D * PROJ_DEV, bytes_accessed=6 * 1024 * 1024, transcendentals=0
        ),
    )(place, doc_row, doc_col, gains, before, *by_y, *in_pieces)


def out_call(layer_no, place, heads, out_pieces):
    return pl.pallas_call(
        functools.partial(out_kernel, layer_no),
        out_shape=[jax.ShapeDtypeStruct((4, HALF, 128), bf16)] * 4,
        in_specs=[SMEM] + [VMEM] * 3,
        out_specs=[VMEM] * 4,
        scratch_shapes=[pltpu.VMEM((4, 256, 512), bf16)],
        compiler_params=PARAMS,
        cost_estimate=pl.CostEstimate(
            flops=TOK * 256 * D, bytes_accessed=4 * 1024 * 1024, transcendentals=0
        ),
    )(place, heads, *out_pieces)


def in_part(core, in_w, rate_w, layer_log, layer_bias, layer_head, norms):
    rates, rows = rate_w.reshape(4, 2, 256, 4), in_w.reshape(4, 2, 256, PROJ_DEV)
    rates, rows = pick(rates, core, 1), pick(rows, core, 1)
    rate_rows = jnp.transpose(rates, (0, 2, 1))
    rate_rows = jnp.pad(rate_rows, ((0, 0), (0, 0), (0, PROJ_DEV - 256)))
    head_row = jnp.pad(layer_head, (0, PROJ_DEV - DV))
    log_row = jnp.pad(layer_log, (2, PROJ_DEV - 4))
    bias_row = jnp.pad(layer_bias, (2, PROJ_DEV - 4))
    norm_rows = jnp.pad(norms, ((0, 0), (0, PROJ_DEV - 128)))
    rest = jnp.concatenate([jnp.stack([head_row, log_row, bias_row]), norm_rows])
    rest = jnp.pad(rest, ((0, 7), (0, 0)))
    rest = jnp.broadcast_to(rest[None], (rows.shape[0], 12, PROJ_DEV))
    return jnp.concatenate([rows, rate_rows, rest], axis=1)


def shards(
    tokens,
    doc_starts,
    owner_map,
    in_weight,
    rate_weight,
    out_weight,
    decay_log,
    decay_bias,
    norm_gain,
    head_gain,
):
    rep, tp = lax.axis_index("rep"), lax.axis_index("tp")
    zh, x, core = rep // 8, (rep // 2) % 4, rep % 2
    y, z = tp // 4, tp % 4
    source = pick(owner_map, tp)
    owner = (source // 8, (source // 2) % 4, source % 2)
    token_pos = jnp.arange(TOK, dtype=jnp.int32)
    doc_ids = jnp.sum((doc_starts[0][None, :] <= token_pos[:, None]).astype(jnp.int32), axis=1)
    by_chunk = doc_ids.reshape(2 * CHUNKS, CHUNK)
    ends = by_chunk[:, -1]
    before = jnp.concatenate([jnp.zeros((1,), jnp.int32), ends[:-1]])
    doc_row = by_chunk.astype(f32)
    empty = jnp.zeros((VH_DEV, DK, DV), f32)
    doc_col = jnp.stack(
        [
            by_chunk.astype(f32),
            (by_chunk == before[:, None]).astype(f32),
            (by_chunk == ends[:, None]).astype(f32),
        ],
        axis=-1,
    ).reshape(TOK, 3)

    place = jnp.stack(
        [((y - t) % 4) * 4 + (z ^ s) for t in range(4) for s in range(4)]
        + [((x - d) % 4) * 2 + (core ^ e) for d in range(4) for e in range(2)]
        + [y, z, core]
    ).astype(jnp.int32)

    owner_zh, owner_x, owner_core = owner
    ours = owner_core == core

    def layer_weights(layer_no):
        return (
            in_weight[0, layer_no],
            rate_weight[0, layer_no],
            decay_log[0, layer_no],
            decay_bias[0, layer_no],
            head_gain[0, layer_no],
            norm_gain[0],
        )

    def back_over_x(current):
        return jnp.stack([current, to_x(current, 1), to_x(current, 3)])

    def out_part(c):
        rows = pick(out_weight[0].reshape(2, 16, 4, 2, 32, 128), c, 3)
        return jnp.transpose(rows, (2, 0, 1, 3, 4))

    by_z = over_z(tokens)
    weights = layer_weights(0)
    half = jnp.where(ours, in_part(core, *weights), other_core(in_part(1 - core, *weights)))
    by_z, half = fence([by_z, half], [])

    current = scatter(half, x, owner_x)
    left, right = to_y(by_z, 1), to_y(by_z, 3)
    out_half = jnp.where(ours, out_part(core), other_core(out_part(1 - core)))
    by_z, current, out_half = fence([by_z, current, out_half], [left, right])

    current = jnp.where(owner_zh == zh, current, other_plane(current))
    across = to_y(by_z, 2)
    out_current = scatter(out_half, x, owner_x)
    current, out_current = fence([current, out_current], [across])
    by_y = [by_z, left, across, right]

    held, held_across = back_over_x(current), to_x(current, 2)[None]
    rows = jnp.where(owner_zh == zh, out_current, other_plane(out_current))
    gains = jnp.pad(current[263:265, 0:128].reshape(2, 1, 1, 128), ((0, 0), (0, 0), (0, 15), (0, 0)))
    rows = jnp.concatenate([rows, jnp.broadcast_to(gains, (2, 16, 16, 128))], axis=2)
    held, held_across, rows = fence([held, held_across, rows], [])

    in_pieces = (held, held_across, other_core(held), other_core(held_across))
    rows = lax.all_to_all(rows, "tp", split_axis=1, concat_axis=1, tiled=True)
    gains = rows[:, :, 32:48]
    (again,) = fence([place], [held])
    weights = layer_weights(1)
    mine, theirs = in_part(again[26], *weights), in_part(1 - again[26], *weights)
    rows, theirs = fence([rows[:, :, 0:32], theirs], [in_pieces[2], in_pieces[3]])

    out_held = jnp.stack([rows] + [to_x(rows, d) for d in (1, 2, 3)])
    late = jnp.where(ours, mine, other_core(theirs))
    docs = (doc_row, doc_col, gains)
    heads, memory = heads_call(0, 0, place, *docs, empty, by_y, in_pieces)
    heads, memory, out_held, late = fence([heads, memory, out_held, late], [])
    out_pieces = (out_held, other_core(out_held))
    late = scatter(late, x, owner_x)
    one = out_call(0, place, heads, out_pieces)

    total, rows = sum_y(one, tokens[0:512])
    heads, _ = heads_call(0, 1, place, *docs, memory, by_y, in_pieces)
    two = out_call(0, place, heads, out_pieces)
    *rows, t0, t1, t2, t3, late = fence([*rows, *two, late], [])
    late = jnp.where(owner_zh == zh, late, other_plane(late))
    stream_one = sum_z(total, rows)
    by_z = over_z(stream_one)
    total, rows = sum_y([t0, t1, t2, t3], tokens[512:])
    by_z, *rows, late = fence([by_z, *rows, late], [])
    groups = [[h * 8 + n for n in range(8)] for h in range(2)]
    in_pieces = [lax.all_gather(late, "rep", axis=0, axis_index_groups=groups)]
    by_y = over_y(by_z)
    stream_two = sum_z(total, rows)
    (by_z,) = fence([over_z(stream_two)], by_y[1:])

    heads, memory = heads_call(1, 0, place, *docs, empty, by_y, in_pieces)
    one = out_call(1, place, heads, out_pieces)
    total, rows = sum_y(one, stream_one)
    heads, _ = heads_call(1, 1, place, *docs, memory, over_y(by_z), in_pieces)
    two = out_call(1, place, heads, out_pieces)
    *rows, t0, t1, t2, t3 = fence([*rows, *two], [])
    stream_one = sum_z(total, rows)
    total, rows = sum_y([t0, t1, t2, t3], stream_two)
    stream_two = sum_z(total, rows)
    return jnp.concatenate([stream_one, stream_two])


def solution(mesh):
    placed = (
        P("rep", "tp"),
        P("rep", None),
        P(),
        P("rep", None, None, "tp"),
        P("rep", None, None, "tp"),
        P("rep", None, None, "tp"),
        P("rep", None, "tp"),
        P("rep", None, "tp"),
        P("rep", None, "tp"),
        P("rep", None, None),
    )
    return jax.shard_map(
        shards, mesh=mesh, in_specs=placed, out_specs=P("rep", "tp"), check_vma=False
    )
```

```python
import functools
import math

import jax
import jax.numpy as jnp
from jax import lax
from jax.experimental import pallas as pl
from jax.experimental.pallas import tpu as pltpu
from jax.sharding import PartitionSpec as P

D = 2048
DK = 128
DV = 128
VH_DEV = 2
PROJ_DEV = 768
TOK = 1024
CHUNK = 128
HALF = TOK // 2
CHUNKS = HALF // CHUNK
GROUP = 4
epsilon = 1e-06

f32 = jnp.float32
bf16 = jnp.bfloat16


def rep_perm(z_shift, x_shift, core_shift):
    pairs = []
    for i in range(16):
        zh, x, c = i // 8, (i // 2) % 4, i % 2
        pairs.append((i, ((zh + z_shift) % 2) * 8 + ((x + x_shift) % 4) * 2 + (c + core_shift) % 2))
    return pairs


def tp_perm(y_shift, z_flip):
    return [(i, ((i // 4 + y_shift) % 4) * 4 + ((i % 4) ^ z_flip)) for i in range(16)]


def pick(array, index, axis=0):
    return lax.dynamic_index_in_dim(array, index, axis, keepdims=False)


def no_work(*refs):
    pass


def fence(values, others):
    anywhere = pl.BlockSpec(memory_space=pl.ANY)
    return pl.pallas_call(
        no_work,
        out_shape=[jax.ShapeDtypeStruct(v.shape, v.dtype) for v in values],
        in_specs=[anywhere] * (len(values) + len(others)),
        out_specs=[anywhere] * len(values),
        input_output_aliases={n: n for n in range(len(values))},
    )(*values, *others)


def to_x(array, d):
    return lax.ppermute(array, "rep", rep_perm(0, d, 0))


def to_y(array, t):
    return lax.ppermute(array, "tp", tp_perm(t, 0))


def to_z(array, s):
    return lax.ppermute(array, "tp", tp_perm(0, s))


def other_plane(array):
    return lax.ppermute(array, "rep", rep_perm(1, 0, 0))


def other_core(array):
    return lax.ppermute(array, "rep", rep_perm(0, 0, 1))


def scatter(half, x, owner_x):
    moved = [to_x(pick(half, (x + d) % 4), d) for d in (1, 2, 3)]
    delta = (x - owner_x) % 4
    current = pick(half, x)
    for d in (1, 2, 3):
        current = jnp.where(delta == d, moved[d - 1], current)
    return current


def over_y(array):
    return [array] + [to_y(array, t) for t in (1, 2, 3)]


def over_z(block):
    return jnp.stack([block] + [to_z(block, s) for s in (1, 2, 3)])


def sum_y(slabs, block):
    came = [slabs[0]] + [to_y(slabs[t], t) for t in (1, 2, 3)]
    total = sum(part[0].astype(f32) for part in came) + block.astype(f32)
    return total, [sum(part[s].astype(f32) for part in came).astype(bf16) for s in (1, 2, 3)]


def sum_z(total, rows):
    for s in (1, 2, 3):
        total = total + to_z(rows[s - 1], s).astype(f32)
    return total.astype(bf16)


def dot(a, b):
    return jnp.dot(a.astype(bf16), b.astype(bf16), preferred_element_type=f32)


def dot_nt(a, b):
    return lax.dot_general(
        a.astype(bf16), b.astype(bf16), (((1,), (1,)), ((), ())), preferred_element_type=f32
    )


def kernel(layer_no, part, place, doc_row, doc_col, gains, before, *refs):
    by_y, in_pieces, heads, memory_out = refs[0:4], refs[4:-13], refs[-13], refs[-12]
    normed, in_w, rate_w, proj, rates, kw, kb, qt, o1, keep, mems = refs[-11:]
    skipped = 0 if layer_no else part * HALF

    rate_w[...] = jnp.zeros_like(rate_w)
    for d in range(4):
        for e in range(2):
            if layer_no:
                p = 2 * d + e
                piece = in_pieces[0].at[p]
            else:
                p = place[16 + 2 * d + e]
                piece = in_pieces[2 * e + 1].at[0] if d == 2 else in_pieces[2 * e].at[(0, 1, None, 2)[d]]
            in_w[pl.ds(pl.multiple_of(p * 256, 256), 256), :] = piece[0:256, :]
            rate_w[0:16, pl.ds(pl.multiple_of(p * 256, 256), 256)] = piece[256:272, 0:256]
    extra = in_pieces[0][0, 256:272, 0:128].astype(f32)
    head_gain = extra[4:5, :]
    log_row = extra[5:6, :]
    bias_row = extra[6:7, :]

    def norm_rows(r, _):
        rows = pl.ds(pl.multiple_of(skipped + r * 128, 128), 128)
        place_rows = pl.ds(pl.multiple_of(r * 128, 128), 128)
        squares = jnp.zeros((128, 128), f32)
        for n in range(16):
            wide = by_y[n // 4][n % 4, rows, :].astype(f32)
            squares = squares + wide * wide
        scale = lax.rsqrt(jnp.sum(squares, axis=1, keepdims=True) / D + epsilon)
        for n in range(16):
            b = place[n]
            gain = gains[layer_no, b].astype(f32)[0:1, :]
            wide = by_y[n // 4][n % 4, rows, :].astype(f32) * scale * gain
            normed[place_rows, pl.ds(pl.multiple_of(b * 128, 128), 128)] = wide.astype(bf16)
        return 0

    lax.fori_loop(0, HALF // 128, norm_rows, 0)

    def project(r, _):
        rows = pl.ds(pl.multiple_of(r * 256, 256), 256)
        left = normed[rows, :]
        proj[rows, :] = jnp.dot(left, in_w[...], preferred_element_type=f32).astype(bf16)
        rates[rows, :] = dot_nt(left, rate_w[...])
        return 0

    lax.fori_loop(0, HALF // 256, project, 0)

    ii = lax.broadcasted_iota(jnp.int32, (CHUNK, CHUNK), 0)
    jj = lax.broadcasted_iota(jnp.int32, (CHUNK, CHUNK), 1)
    eye = (ii == jj).astype(f32)
    inclusive = ii >= jj

    def prepare(group, _):
        lowers, solved, scores, rights, tails, lasts, queries, carries = [], [], [], [], [], [], [], []
        for n in range(GROUP):
            c = group * GROUP + n
            rows = pl.ds(pl.multiple_of(c * CHUNK, CHUNK), CHUNK)
            query = proj[rows, 0:128].astype(f32)
            key = proj[rows, 128:256].astype(f32)
            query = query * (
                lax.rsqrt(jnp.sum(query * query, axis=1, keepdims=True) + epsilon) / math.sqrt(DK)
            )
            key = key * lax.rsqrt(jnp.sum(key * key, axis=1, keepdims=True) + epsilon)
            key_gram = dot_nt(key, key)
            query_gram = dot_nt(query, key)
            raw = rates[rows, :]
            beta = 1.0 / (1.0 + jnp.exp(-raw))
            moved = raw + bias_row
            soft = jnp.maximum(moved, 0.0) + jnp.log1p(jnp.exp(-jnp.abs(moved)))
            decay = -jnp.exp(log_row) * soft
            cumulative = jnp.dot(
                inclusive.astype(f32), decay, preferred_element_type=f32, precision=lax.Precision.HIGHEST
            )
            across = cumulative.T
            docs = doc_col[pl.ds(pl.multiple_of(part * HALF + c * CHUNK, CHUNK), CHUNK), :]
            same = docs[:, 0:1] == doc_row[pl.ds(part * CHUNKS + c, 1), :]
            kept = jnp.logical_and(same, inclusive)
            for h in range(VH_DEV):
                cum = cumulative[:, 2 + h : 3 + h]
                pair = jnp.where(
                    kept, jnp.exp(jnp.minimum(cum - across[2 + h : 3 + h, :], 0.0)), 0.0
                )
                carried = jnp.exp(cum) * docs[:, 1:2]
                rate = beta[:, h : h + 1]
                tail = jnp.exp(jnp.minimum(cum[CHUNK - 1 :, :] - cum, 0.0)) * docs[:, 2:3]
                lower = jnp.where(ii > jj, rate * key_gram * pair, 0.0)
                lowers.append(lower.astype(bf16))
                solved.append(eye - jnp.where(ii // 2 == jj // 2, lower, 0.0))
                scores.append((query_gram * pair).astype(bf16))
                value = proj[rows, 256 + h * 128 : 384 + h * 128].astype(f32)
                rights.append(
                    jnp.concatenate(
                        [(rate * value).astype(bf16), (rate * carried * key).astype(bf16)], axis=1
                    )
                )
                tails.append((key * tail).T.astype(bf16))
                lasts.append(carried[CHUNK - 1 :, :])
                queries.append(carried * query)
        size = 2
        while size < CHUNK:
            corner = jnp.logical_and(
                ii // (2 * size) == jj // (2 * size),
                jnp.logical_and((ii // size) % 2 == 1, (jj // size) % 2 == 0),
            )
            halves = []
            for n in range(len(lowers)):
                halves.append(dot(jnp.where(corner, lowers[n], jnp.zeros_like(lowers[n])), solved[n]))
            for n in range(len(lowers)):
                solved[n] = solved[n] - dot(solved[n], halves[n])
            size *= 2
        updates = [dot(solved[n], rights[n]).astype(bf16) for n in range(len(lowers))]
        for n in range(len(lowers)):
            m = group * GROUP * VH_DEV + n
            through = dot(scores[n], updates[n])
            o1[m] = through[:, 0:128]
            qt[m] = (queries[n] - through[:, 128:256]).astype(bf16)
            stored = dot(tails[n], updates[n])
            kb[m] = stored[:, 0:128]
            kw[m] = stored[:, 128:256].astype(bf16)
            keep[m] = jnp.broadcast_to(lasts[n], (8, 128))
        return 0

    lax.fori_loop(0, CHUNKS // GROUP, prepare, 0)

    memory = [before[h] for h in range(VH_DEV)]
    for c in range(CHUNKS):
        for h in range(VH_DEV):
            m = c * VH_DEV + h
            narrow = memory[h].astype(bf16)
            mems[m] = narrow
            if c < CHUNKS - 1 or part == 0:
                memory[h] = keep[m][0:1, :] * memory[h] + (kb[m] - dot(kw[m], narrow))

    for h in range(VH_DEV):
        memory_out[h] = memory[h]

    def finish(c, _):
        rows = pl.ds(pl.multiple_of(c * CHUNK, CHUNK), CHUNK)
        for h in range(VH_DEV):
            m = c * VH_DEV + h
            mixed = o1[m] + dot(qt[m], mems[m])
            scaled = mixed * lax.rsqrt(jnp.mean(mixed * mixed, axis=1, keepdims=True) + epsilon)
            gate = proj[rows, 512 + h * 128 : 640 + h * 128].astype(f32)
            scaled = scaled * head_gain * (gate / (1.0 + jnp.exp(-gate)))
            heads[rows, h * 128 : (h + 1) * 128] = scaled.astype(bf16)
        return 0

    lax.fori_loop(0, CHUNKS, finish, 0)


def out_kernel(layer_no, place, heads, held, sibling, *refs):
    slabs, out_w = refs[0:4], refs[4]
    y, z = place[24], place[25]
    for d in range(4):
        for e in range(2):
            rows = pl.ds(pl.multiple_of(place[16 + 2 * d + e] * 32, 32), 32)
            for c in range(16):
                columns = pl.ds(pl.multiple_of(((c % 4) ^ z) * 128, 128), 128)
                out_w[(c // 4 + 4 - y) % 4, rows, columns] = (held, sibling)[e][d, layer_no, c]

    def outputs(r, _):
        rows = pl.ds(pl.multiple_of(r * 256, 256), 256)
        left = heads[rows, :]
        for t in range(4):
            made = jnp.dot(left, out_w[t], preferred_element_type=f32).astype(bf16)
            for s in range(4):
                slabs[t][s, rows, :] = made[:, s * 128 : (s + 1) * 128]
        return 0

    lax.fori_loop(0, HALF // 256, outputs, 0)


VMEM = pl.BlockSpec(memory_space=pltpu.VMEM)
SMEM = pl.BlockSpec(memory_space=pltpu.SMEM)
PARAMS = pltpu.CompilerParams(vmem_limit_bytes=56 * 1024 * 1024)


def heads_call(layer_no, part, place, doc_row, doc_col, gains, before, by_y, in_pieces):
    return pl.pallas_call(
        functools.partial(kernel, layer_no, part),
        out_shape=[
            jax.ShapeDtypeStruct((HALF, 256), bf16),
            jax.ShapeDtypeStruct((VH_DEV, DK, DV), f32),
        ],
        in_specs=[SMEM] + [VMEM] * (4 + len(by_y) + len(in_pieces)),
        out_specs=[VMEM] * 2,
        scratch_shapes=[
            pltpu.VMEM((HALF, D), bf16),
            pltpu.VMEM((D, PROJ_DEV), bf16),
            pltpu.VMEM((128, D), bf16),
            pltpu.VMEM((HALF, PROJ_DEV), bf16),
            pltpu.VMEM((HALF, 128), f32),
            pltpu.VMEM((8, 128, 128), bf16),
            pltpu.VMEM((8, 128, 128), f32),
            pltpu.VMEM((8, 128, 128), bf16),
            pltpu.VMEM((8, 128, 128), f32),
            pltpu.VMEM((8, 8, 128), f32),
            pltpu.VMEM((8, 128, 128), bf16),
        ],
        compiler_params=PARAMS,
        cost_estimate=pl.CostEstimate(
            flops=4 * TOK * D * PROJ_DEV, bytes_accessed=6 * 1024 * 1024, transcendentals=0
        ),
    )(place, doc_row, doc_col, gains, before, *by_y, *in_pieces)


def out_call(layer_no, place, heads, out_pieces):
    return pl.pallas_call(
        functools.partial(out_kernel, layer_no),
        out_shape=[jax.ShapeDtypeStruct((4, HALF, 128), bf16)] * 4,
        in_specs=[SMEM] + [VMEM] * 3,
        out_specs=[VMEM] * 4,
        scratch_shapes=[pltpu.VMEM((4, 256, 512), bf16)],
        compiler_params=PARAMS,
        cost_estimate=pl.CostEstimate(
            flops=TOK * 256 * D, bytes_accessed=4 * 1024 * 1024, transcendentals=0
        ),
    )(place, heads, *out_pieces)


def in_part(core, in_w, rate_w, layer_log, layer_bias, layer_head, norms):
    rates, rows = rate_w.reshape(4, 2, 256, 4), in_w.reshape(4, 2, 256, PROJ_DEV)
    rates, rows = pick(rates, core, 1), pick(rows, core, 1)
    rate_rows = jnp.transpose(rates, (0, 2, 1))
    rate_rows = jnp.pad(rate_rows, ((0, 0), (0, 0), (0, PROJ_DEV - 256)))
    head_row = jnp.pad(layer_head, (0, PROJ_DEV - DV))
    log_row = jnp.pad(layer_log, (2, PROJ_DEV - 4))
    bias_row = jnp.pad(layer_bias, (2, PROJ_DEV - 4))
    norm_rows = jnp.pad(norms, ((0, 0), (0, PROJ_DEV - 128)))
    rest = jnp.concatenate([jnp.stack([head_row, log_row, bias_row]), norm_rows])
    rest = jnp.pad(rest, ((0, 7), (0, 0)))
    rest = jnp.broadcast_to(rest[None], (rows.shape[0], 12, PROJ_DEV))
    return jnp.concatenate([rows, rate_rows, rest], axis=1)


def shards(
    tokens,
    doc_starts,
    owner_map,
    in_weight,
    rate_weight,
    out_weight,
    decay_log,
    decay_bias,
    norm_gain,
    head_gain,
):
    rep, tp = lax.axis_index("rep"), lax.axis_index("tp")
    zh, x, core = rep // 8, (rep // 2) % 4, rep % 2
    y, z = tp // 4, tp % 4
    source = pick(owner_map, tp)
    owner = (source // 8, (source // 2) % 4, source % 2)
    token_pos = jnp.arange(TOK, dtype=jnp.int32)
    doc_ids = jnp.sum((doc_starts[0][None, :] <= token_pos[:, None]).astype(jnp.int32), axis=1)
    by_chunk = doc_ids.reshape(2 * CHUNKS, CHUNK)
    ends = by_chunk[:, -1]
    before = jnp.concatenate([jnp.zeros((1,), jnp.int32), ends[:-1]])
    doc_row = by_chunk.astype(f32)
    empty = jnp.zeros((VH_DEV, DK, DV), f32)
    doc_col = jnp.stack(
        [
            by_chunk.astype(f32),
            (by_chunk == before[:, None]).astype(f32),
            (by_chunk == ends[:, None]).astype(f32),
        ],
        axis=-1,
    ).reshape(TOK, 3)

    place = jnp.stack(
        [((y - t) % 4) * 4 + (z ^ s) for t in range(4) for s in range(4)]
        + [((x - d) % 4) * 2 + (core ^ e) for d in range(4) for e in range(2)]
        + [y, z, core]
    ).astype(jnp.int32)

    owner_zh, owner_x, owner_core = owner
    ours = owner_core == core

    def layer_weights(layer_no):
        return (
            in_weight[0, layer_no],
            rate_weight[0, layer_no],
            decay_log[0, layer_no],
            decay_bias[0, layer_no],
            head_gain[0, layer_no],
            norm_gain[0],
        )

    def back_over_x(current):
        return jnp.stack([current, to_x(current, 1), to_x(current, 3)])

    def out_part(c):
        rows = pick(out_weight[0].reshape(2, 16, 4, 2, 32, 128), c, 3)
        return jnp.transpose(rows, (2, 0, 1, 3, 4))

    by_z = over_z(tokens)
    weights = layer_weights(0)
    half = jnp.where(ours, in_part(core, *weights), other_core(in_part(1 - core, *weights)))
    by_z, half = fence([by_z, half], [])

    current = scatter(half, x, owner_x)
    left, right = to_y(by_z, 1), to_y(by_z, 3)
    out_half = jnp.where(ours, out_part(core), other_core(out_part(1 - core)))
    by_z, current, out_half, again = fence([by_z, current, out_half, place], [left, right])

    current = jnp.where(owner_zh == zh, current, other_plane(current))
    across = to_y(by_z, 2)
    out_current = scatter(out_half, x, owner_x)
    weights = layer_weights(1)
    mine, theirs = in_part(again[26], *weights), in_part(1 - again[26], *weights)
    current, out_current, theirs = fence([current, out_current, theirs], [across])
    by_y = [by_z, left, across, right]

    held, held_across = back_over_x(current), to_x(current, 2)[None]
    rows = jnp.where(owner_zh == zh, out_current, other_plane(out_current))
    gains = jnp.pad(current[263:265, 0:128].reshape(2, 1, 1, 128), ((0, 0), (0, 0), (0, 15), (0, 0)))
    rows = jnp.concatenate([rows, jnp.broadcast_to(gains, (2, 16, 16, 128))], axis=2)
    late = jnp.where(ours, mine, other_core(theirs))
    held, held_across, rows, late = fence([held, held_across, rows, late], [])

    in_pieces = (held, held_across, other_core(held), other_core(held_across))
    rows = lax.all_to_all(rows, "tp", split_axis=1, concat_axis=1, tiled=True)
    gains = rows[:, :, 32:48]
    late = scatter(late, x, owner_x)
    rows, late = fence([rows[:, :, 0:32], late], [in_pieces[2], in_pieces[3]])

    out_held = jnp.stack([rows] + [to_x(rows, d) for d in (1, 2, 3)])
    late = jnp.where(owner_zh == zh, late, other_plane(late))
    docs = (doc_row, doc_col, gains)
    heads, memory = heads_call(0, 0, place, *docs, empty, by_y, in_pieces)
    heads, memory, out_held, late = fence([heads, memory, out_held, late], [])
    out_pieces = (out_held, other_core(out_held))
    one = out_call(0, place, heads, out_pieces)

    total, rows = sum_y(one, tokens[0:512])
    heads, _ = heads_call(0, 1, place, *docs, memory, by_y, in_pieces)
    two = out_call(0, place, heads, out_pieces)
    *rows, t0, t1, t2, t3, late = fence([*rows, *two, late], [])
    stream_one = sum_z(total, rows)
    by_z = over_z(stream_one)
    total, rows = sum_y([t0, t1, t2, t3], tokens[512:])
    by_z, *rows = fence([by_z, *rows], [])
    groups = [[h * 8 + n for n in range(8)] for h in range(2)]
    in_pieces = [lax.all_gather(late, "rep", axis=0, axis_index_groups=groups)]
    by_y = over_y(by_z)
    stream_two = sum_z(total, rows)
    (by_z,) = fence([over_z(stream_two)], by_y[1:])

    heads, memory = heads_call(1, 0, place, *docs, empty, by_y, in_pieces)
    one = out_call(1, place, heads, out_pieces)
    total, rows = sum_y(one, stream_one)
    heads, _ = heads_call(1, 1, place, *docs, memory, over_y(by_z), in_pieces)
    two = out_call(1, place, heads, out_pieces)
    *rows, t0, t1, t2, t3 = fence([*rows, *two], [])
    stream_one = sum_z(total, rows)
    total, rows = sum_y([t0, t1, t2, t3], stream_two)
    stream_two = sum_z(total, rows)
    return jnp.concatenate([stream_one, stream_two])


def solution(mesh):
    placed = (
        P("rep", "tp"),
        P("rep", None),
        P(),
        P("rep", None, None, "tp"),
        P("rep", None, None, "tp"),
        P("rep", None, None, "tp"),
        P("rep", None, "tp"),
        P("rep", None, "tp"),
        P("rep", None, "tp"),
        P("rep", None, None),
    )
    return jax.shard_map(
        shards, mesh=mesh, in_specs=placed, out_specs=P("rep", "tp"), check_vma=False
    )
```

```python
import functools
import math

import jax
import jax.numpy as jnp
from jax import lax
from jax.experimental import pallas as pl
from jax.experimental.pallas import tpu as pltpu
from jax.sharding import PartitionSpec as P

D = 2048
DK = 128
DV = 128
VH_DEV = 2
PROJ_DEV = 768
TOK = 1024
CHUNK = 128
HALF = TOK // 2
CHUNKS = HALF // CHUNK
GROUP = 4
epsilon = 1e-06

f32 = jnp.float32
bf16 = jnp.bfloat16


def rep_perm(z_shift, x_shift, core_shift):
    pairs = []
    for i in range(16):
        zh, x, c = i // 8, (i // 2) % 4, i % 2
        pairs.append((i, ((zh + z_shift) % 2) * 8 + ((x + x_shift) % 4) * 2 + (c + core_shift) % 2))
    return pairs


def tp_perm(y_shift, z_flip):
    return [(i, ((i // 4 + y_shift) % 4) * 4 + ((i % 4) ^ z_flip)) for i in range(16)]


def pick(array, index, axis=0):
    return lax.dynamic_index_in_dim(array, index, axis, keepdims=False)


def no_work(*refs):
    pass


def fence(values, others):
    anywhere = pl.BlockSpec(memory_space=pl.ANY)
    return pl.pallas_call(
        no_work,
        out_shape=[jax.ShapeDtypeStruct(v.shape, v.dtype) for v in values],
        in_specs=[anywhere] * (len(values) + len(others)),
        out_specs=[anywhere] * len(values),
        input_output_aliases={n: n for n in range(len(values))},
    )(*values, *others)


def to_x(array, d):
    return lax.ppermute(array, "rep", rep_perm(0, d, 0))


def to_y(array, t):
    return lax.ppermute(array, "tp", tp_perm(t, 0))


def to_z(array, s):
    return lax.ppermute(array, "tp", tp_perm(0, s))


def other_plane(array):
    return lax.ppermute(array, "rep", rep_perm(1, 0, 0))


def other_core(array):
    return lax.ppermute(array, "rep", rep_perm(0, 0, 1))


def scatter(half, x, owner_x):
    moved = [to_x(pick(half, (x + d) % 4), d) for d in (1, 2, 3)]
    delta = (x - owner_x) % 4
    current = pick(half, x)
    for d in (1, 2, 3):
        current = jnp.where(delta == d, moved[d - 1], current)
    return current


def over_y(array):
    return [array] + [to_y(array, t) for t in (1, 2, 3)]


def over_z(block):
    return jnp.stack([block] + [to_z(block, s) for s in (1, 2, 3)])


def sum_y(slabs, block):
    came = [slabs[0]] + [to_y(slabs[t], t) for t in (1, 2, 3)]
    total = sum(part[0].astype(f32) for part in came) + block.astype(f32)
    return total, [sum(part[s].astype(f32) for part in came).astype(bf16) for s in (1, 2, 3)]


def sum_z(total, rows):
    for s in (1, 2, 3):
        total = total + to_z(rows[s - 1], s).astype(f32)
    return total.astype(bf16)


def dot(a, b):
    return jnp.dot(a.astype(bf16), b.astype(bf16), preferred_element_type=f32)


def dot_nt(a, b):
    return lax.dot_general(
        a.astype(bf16), b.astype(bf16), (((1,), (1,)), ((), ())), preferred_element_type=f32
    )


def kernel(layer_no, part, place, doc_row, doc_col, gains, before, *refs):
    by_y, in_pieces, heads, memory_out = refs[0:4], refs[4:-13], refs[-13], refs[-12]
    normed, in_w, rate_w, proj, rates, kw, kb, qt, o1, keep, mems = refs[-11:]
    skipped = 0 if layer_no else part * HALF

    rate_w[...] = jnp.zeros_like(rate_w)
    for d in range(4):
        for e in range(2):
            if layer_no:
                p = 2 * d + e
                piece = in_pieces[0].at[p]
            else:
                p = place[16 + 2 * d + e]
                piece = in_pieces[2 * e + 1].at[0] if d == 2 else in_pieces[2 * e].at[(0, 1, None, 2)[d]]
            in_w[pl.ds(pl.multiple_of(p * 256, 256), 256), :] = piece[0:256, :]
            rate_w[0:16, pl.ds(pl.multiple_of(p * 256, 256), 256)] = piece[256:272, 0:256]
    extra = in_pieces[0][0, 256:272, 0:128].astype(f32)
    head_gain = extra[4:5, :]
    log_row = extra[5:6, :]
    bias_row = extra[6:7, :]

    def norm_rows(r, _):
        rows = pl.ds(pl.multiple_of(skipped + r * 128, 128), 128)
        place_rows = pl.ds(pl.multiple_of(r * 128, 128), 128)
        squares = jnp.zeros((128, 128), f32)
        for n in range(16):
            wide = by_y[n // 4][n % 4, rows, :].astype(f32)
            squares = squares + wide * wide
        scale = lax.rsqrt(jnp.sum(squares, axis=1, keepdims=True) / D + epsilon)
        for n in range(16):
            b = place[n]
            gain = gains[layer_no, b].astype(f32)[0:1, :]
            wide = by_y[n // 4][n % 4, rows, :].astype(f32) * scale * gain
            normed[place_rows, pl.ds(pl.multiple_of(b * 128, 128), 128)] = wide.astype(bf16)
        return 0

    lax.fori_loop(0, HALF // 128, norm_rows, 0)

    def project(r, _):
        rows = pl.ds(pl.multiple_of(r * 256, 256), 256)
        left = normed[rows, :]
        proj[rows, :] = jnp.dot(left, in_w[...], preferred_element_type=f32).astype(bf16)
        rates[rows, :] = dot_nt(left, rate_w[...])
        return 0

    lax.fori_loop(0, HALF // 256, project, 0)

    ii = lax.broadcasted_iota(jnp.int32, (CHUNK, CHUNK), 0)
    jj = lax.broadcasted_iota(jnp.int32, (CHUNK, CHUNK), 1)
    eye = (ii == jj).astype(f32)
    inclusive = ii >= jj

    def prepare(group, _):
        lowers, solved, scores, rights, tails, lasts, queries, carries = [], [], [], [], [], [], [], []
        for n in range(GROUP):
            c = group * GROUP + n
            rows = pl.ds(pl.multiple_of(c * CHUNK, CHUNK), CHUNK)
            query = proj[rows, 0:128].astype(f32)
            key = proj[rows, 128:256].astype(f32)
            query = query * (
                lax.rsqrt(jnp.sum(query * query, axis=1, keepdims=True) + epsilon) / math.sqrt(DK)
            )
            key = key * lax.rsqrt(jnp.sum(key * key, axis=1, keepdims=True) + epsilon)
            key_gram = dot_nt(key, key)
            query_gram = dot_nt(query, key)
            raw = rates[rows, :]
            beta = 1.0 / (1.0 + jnp.exp(-raw))
            moved = raw + bias_row
            soft = jnp.maximum(moved, 0.0) + jnp.log1p(jnp.exp(-jnp.abs(moved)))
            decay = -jnp.exp(log_row) * soft
            cumulative = jnp.dot(
                inclusive.astype(f32), decay, preferred_element_type=f32, precision=lax.Precision.HIGHEST
            )
            across = cumulative.T
            docs = doc_col[pl.ds(pl.multiple_of(part * HALF + c * CHUNK, CHUNK), CHUNK), :]
            same = docs[:, 0:1] == doc_row[pl.ds(part * CHUNKS + c, 1), :]
            kept = jnp.logical_and(same, inclusive)
            for h in range(VH_DEV):
                cum = cumulative[:, 2 + h : 3 + h]
                pair = jnp.where(
                    kept, jnp.exp(jnp.minimum(cum - across[2 + h : 3 + h, :], 0.0)), 0.0
                )
                carried = jnp.exp(cum) * docs[:, 1:2]
                rate = beta[:, h : h + 1]
                tail = jnp.exp(jnp.minimum(cum[CHUNK - 1 :, :] - cum, 0.0)) * docs[:, 2:3]
                lower = jnp.where(ii > jj, rate * key_gram * pair, 0.0)
                lowers.append(lower.astype(bf16))
                solved.append(eye - jnp.where(ii // 2 == jj // 2, lower, 0.0))
                scores.append((query_gram * pair).astype(bf16))
                value = proj[rows, 256 + h * 128 : 384 + h * 128].astype(f32)
                rights.append(
                    jnp.concatenate(
                        [(rate * value).astype(bf16), (rate * carried * key).astype(bf16)], axis=1
                    )
                )
                tails.append((key * tail).T.astype(bf16))
                lasts.append(carried[CHUNK - 1 :, :])
                queries.append(carried * query)
        size = 2
        while size < CHUNK:
            corner = jnp.logical_and(
                ii // (2 * size) == jj // (2 * size),
                jnp.logical_and((ii // size) % 2 == 1, (jj // size) % 2 == 0),
            )
            halves = []
            for n in range(len(lowers)):
                halves.append(dot(jnp.where(corner, lowers[n], jnp.zeros_like(lowers[n])), solved[n]))
            for n in range(len(lowers)):
                solved[n] = solved[n] - dot(solved[n], halves[n])
            size *= 2
        updates = [dot(solved[n], rights[n]).astype(bf16) for n in range(len(lowers))]
        for n in range(len(lowers)):
            m = group * GROUP * VH_DEV + n
            through = dot(scores[n], updates[n])
            o1[m] = through[:, 0:128]
            qt[m] = (queries[n] - through[:, 128:256]).astype(bf16)
            stored = dot(tails[n], updates[n])
            kb[m] = stored[:, 0:128]
            kw[m] = stored[:, 128:256].astype(bf16)
            keep[m] = jnp.broadcast_to(lasts[n], (8, 128))
        return 0

    lax.fori_loop(0, CHUNKS // GROUP, prepare, 0)

    memory = [before[h] for h in range(VH_DEV)]
    for c in range(CHUNKS):
        for h in range(VH_DEV):
            m = c * VH_DEV + h
            narrow = memory[h].astype(bf16)
            mems[m] = narrow
            if c < CHUNKS - 1 or part == 0:
                memory[h] = keep[m][0:1, :] * memory[h] + (kb[m] - dot(kw[m], narrow))

    for h in range(VH_DEV):
        memory_out[h] = memory[h]

    def finish(c, _):
        rows = pl.ds(pl.multiple_of(c * CHUNK, CHUNK), CHUNK)
        for h in range(VH_DEV):
            m = c * VH_DEV + h
            mixed = o1[m] + dot(qt[m], mems[m])
            scaled = mixed * lax.rsqrt(jnp.mean(mixed * mixed, axis=1, keepdims=True) + epsilon)
            gate = proj[rows, 512 + h * 128 : 640 + h * 128].astype(f32)
            scaled = scaled * head_gain * (gate / (1.0 + jnp.exp(-gate)))
            heads[rows, h * 128 : (h + 1) * 128] = scaled.astype(bf16)
        return 0

    lax.fori_loop(0, CHUNKS, finish, 0)


def out_kernel(layer_no, place, heads, held, sibling, *refs):
    slabs, out_w = refs[0:4], refs[4]
    y, z = place[24], place[25]
    for d in range(4):
        for e in range(2):
            rows = pl.ds(pl.multiple_of(place[16 + 2 * d + e] * 32, 32), 32)
            for c in range(16):
                columns = pl.ds(pl.multiple_of(((c % 4) ^ z) * 128, 128), 128)
                out_w[(c // 4 + 4 - y) % 4, rows, columns] = (held, sibling)[e][d, layer_no, c]

    def outputs(r, _):
        rows = pl.ds(pl.multiple_of(r * 256, 256), 256)
        left = heads[rows, :]
        for t in range(4):
            made = jnp.dot(left, out_w[t], preferred_element_type=f32).astype(bf16)
            for s in range(4):
                slabs[t][s, rows, :] = made[:, s * 128 : (s + 1) * 128]
        return 0

    lax.fori_loop(0, HALF // 256, outputs, 0)


VMEM = pl.BlockSpec(memory_space=pltpu.VMEM)
SMEM = pl.BlockSpec(memory_space=pltpu.SMEM)
PARAMS = pltpu.CompilerParams(vmem_limit_bytes=56 * 1024 * 1024)


def heads_call(layer_no, part, place, doc_row, doc_col, gains, before, by_y, in_pieces):
    return pl.pallas_call(
        functools.partial(kernel, layer_no, part),
        out_shape=[
            jax.ShapeDtypeStruct((HALF, 256), bf16),
            jax.ShapeDtypeStruct((VH_DEV, DK, DV), f32),
        ],
        in_specs=[SMEM] + [VMEM] * (4 + len(by_y) + len(in_pieces)),
        out_specs=[VMEM] * 2,
        scratch_shapes=[
            pltpu.VMEM((HALF, D), bf16),
            pltpu.VMEM((D, PROJ_DEV), bf16),
            pltpu.VMEM((128, D), bf16),
            pltpu.VMEM((HALF, PROJ_DEV), bf16),
            pltpu.VMEM((HALF, 128), f32),
            pltpu.VMEM((8, 128, 128), bf16),
            pltpu.VMEM((8, 128, 128), f32),
            pltpu.VMEM((8, 128, 128), bf16),
            pltpu.VMEM((8, 128, 128), f32),
            pltpu.VMEM((8, 8, 128), f32),
            pltpu.VMEM((8, 128, 128), bf16),
        ],
        compiler_params=PARAMS,
        cost_estimate=pl.CostEstimate(
            flops=4 * TOK * D * PROJ_DEV, bytes_accessed=6 * 1024 * 1024, transcendentals=0
        ),
    )(place, doc_row, doc_col, gains, before, *by_y, *in_pieces)


def out_call(layer_no, place, heads, out_pieces):
    return pl.pallas_call(
        functools.partial(out_kernel, layer_no),
        out_shape=[jax.ShapeDtypeStruct((4, HALF, 128), bf16)] * 4,
        in_specs=[SMEM] + [VMEM] * 3,
        out_specs=[VMEM] * 4,
        scratch_shapes=[pltpu.VMEM((4, 256, 512), bf16)],
        compiler_params=PARAMS,
        cost_estimate=pl.CostEstimate(
            flops=TOK * 256 * D, bytes_accessed=4 * 1024 * 1024, transcendentals=0
        ),
    )(place, heads, *out_pieces)


def in_part(core, in_w, rate_w, layer_log, layer_bias, layer_head, norms):
    rates, rows = rate_w.reshape(4, 2, 256, 4), in_w.reshape(4, 2, 256, PROJ_DEV)
    rates, rows = pick(rates, core, 1), pick(rows, core, 1)
    rate_rows = jnp.transpose(rates, (0, 2, 1))
    rate_rows = jnp.pad(rate_rows, ((0, 0), (0, 0), (0, PROJ_DEV - 256)))
    head_row = jnp.pad(layer_head, (0, PROJ_DEV - DV))
    log_row = jnp.pad(layer_log, (2, PROJ_DEV - 4))
    bias_row = jnp.pad(layer_bias, (2, PROJ_DEV - 4))
    norm_rows = jnp.pad(norms, ((0, 0), (0, PROJ_DEV - 128)))
    rest = jnp.concatenate([jnp.stack([head_row, log_row, bias_row]), norm_rows])
    rest = jnp.pad(rest, ((0, 7), (0, 0)))
    rest = jnp.broadcast_to(rest[None], (rows.shape[0], 12, PROJ_DEV))
    return jnp.concatenate([rows, rate_rows, rest], axis=1)


def shards(
    tokens,
    doc_starts,
    owner_map,
    in_weight,
    rate_weight,
    out_weight,
    decay_log,
    decay_bias,
    norm_gain,
    head_gain,
):
    rep, tp = lax.axis_index("rep"), lax.axis_index("tp")
    zh, x, core = rep // 8, (rep // 2) % 4, rep % 2
    y, z = tp // 4, tp % 4
    source = pick(owner_map, tp)
    owner = (source // 8, (source // 2) % 4, source % 2)
    token_pos = jnp.arange(TOK, dtype=jnp.int32)
    doc_ids = jnp.sum((doc_starts[0][None, :] <= token_pos[:, None]).astype(jnp.int32), axis=1)
    by_chunk = doc_ids.reshape(2 * CHUNKS, CHUNK)
    ends = by_chunk[:, -1]
    before = jnp.concatenate([jnp.zeros((1,), jnp.int32), ends[:-1]])
    doc_row = by_chunk.astype(f32)
    empty = jnp.zeros((VH_DEV, DK, DV), f32)
    doc_col = jnp.stack(
        [
            by_chunk.astype(f32),
            (by_chunk == before[:, None]).astype(f32),
            (by_chunk == ends[:, None]).astype(f32),
        ],
        axis=-1,
    ).reshape(TOK, 3)

    place = jnp.stack(
        [((y - t) % 4) * 4 + (z ^ s) for t in range(4) for s in range(4)]
        + [((x - d) % 4) * 2 + (core ^ e) for d in range(4) for e in range(2)]
        + [y, z, core]
    ).astype(jnp.int32)

    owner_zh, owner_x, owner_core = owner
    ours = owner_core == core

    def layer_weights(layer_no):
        return (
            in_weight[0, layer_no],
            rate_weight[0, layer_no],
            decay_log[0, layer_no],
            decay_bias[0, layer_no],
            head_gain[0, layer_no],
            norm_gain[0],
        )

    def back_over_x(current):
        return jnp.stack([current, to_x(current, 1), to_x(current, 3)])

    def out_part(c):
        rows = pick(out_weight[0].reshape(2, 16, 4, 2, 32, 128), c, 3)
        return jnp.transpose(rows, (2, 0, 1, 3, 4))

    by_z = over_z(tokens)
    weights = layer_weights(0)
    half = jnp.where(ours, in_part(core, *weights), other_core(in_part(1 - core, *weights)))
    by_z, half = fence([by_z, half], [])

    current = scatter(half, x, owner_x)
    left, right = to_y(by_z, 1), to_y(by_z, 3)
    out_half = jnp.where(ours, out_part(core), other_core(out_part(1 - core)))
    by_z, current, out_half, again = fence([by_z, current, out_half, place], [left, right])

    current = jnp.where(owner_zh == zh, current, other_plane(current))
    across = to_y(by_z, 2)
    out_current = scatter(out_half, x, owner_x)
    weights = layer_weights(1)
    mine, theirs = in_part(again[26], *weights), in_part(1 - again[26], *weights)
    current, out_current, theirs = fence([current, out_current, theirs], [across])
    by_y = [by_z, left, across, right]

    held, held_across = back_over_x(current), to_x(current, 2)[None]
    rows = jnp.where(owner_zh == zh, out_current, other_plane(out_current))
    gains = jnp.pad(current[263:265, 0:128].reshape(2, 1, 1, 128), ((0, 0), (0, 0), (0, 15), (0, 0)))
    rows = jnp.concatenate([rows, jnp.broadcast_to(gains, (2, 16, 16, 128))], axis=2)
    late = jnp.where(ours, mine, other_core(theirs))
    held, held_across, rows, late = fence([held, held_across, rows, late], [])

    in_pieces = (held, held_across, other_core(held), other_core(held_across))
    rows = lax.all_to_all(rows, "tp", split_axis=1, concat_axis=1, tiled=True)
    gains = rows[:, :, 32:48]
    (late,) = fence([late], [in_pieces[3]])
    late = scatter(late, x, owner_x)
    rows, late = fence([rows[:, :, 0:32], late], [in_pieces[2], in_pieces[3]])

    out_held = jnp.stack([rows] + [to_x(rows, d) for d in (1, 2, 3)])
    late = jnp.where(owner_zh == zh, late, other_plane(late))
    docs = (doc_row, doc_col, gains)
    heads, memory = heads_call(0, 0, place, *docs, empty, by_y, in_pieces)
    heads, memory, out_held, late = fence([heads, memory, out_held, late], [])
    out_pieces = (out_held, other_core(out_held))
    one = out_call(0, place, heads, out_pieces)

    total, rows = sum_y(one, tokens[0:512])
    heads, _ = heads_call(0, 1, place, *docs, memory, by_y, in_pieces)
    two = out_call(0, place, heads, out_pieces)
    *rows, t0, t1, t2, t3, late = fence([*rows, *two, late], [])
    stream_one = sum_z(total, rows)
    by_z = over_z(stream_one)
    total, rows = sum_y([t0, t1, t2, t3], tokens[512:])
    by_z, *rows = fence([by_z, *rows], [])
    groups = [[h * 8 + n for n in range(8)] for h in range(2)]
    in_pieces = [lax.all_gather(late, "rep", axis=0, axis_index_groups=groups)]
    by_y = over_y(by_z)
    stream_two = sum_z(total, rows)
    (by_z,) = fence([over_z(stream_two)], by_y[1:])

    heads, memory = heads_call(1, 0, place, *docs, empty, by_y, in_pieces)
    one = out_call(1, place, heads, out_pieces)
    total, rows = sum_y(one, stream_one)
    heads, _ = heads_call(1, 1, place, *docs, memory, over_y(by_z), in_pieces)
    two = out_call(1, place, heads, out_pieces)
    *rows, t0, t1, t2, t3 = fence([*rows, *two], [])
    stream_one = sum_z(total, rows)
    total, rows = sum_y([t0, t1, t2, t3], stream_two)
    stream_two = sum_z(total, rows)
    return jnp.concatenate([stream_one, stream_two])


def solution(mesh):
    placed = (
        P("rep", "tp"),
        P("rep", None),
        P(),
        P("rep", None, None, "tp"),
        P("rep", None, None, "tp"),
        P("rep", None, None, "tp"),
        P("rep", None, "tp"),
        P("rep", None, "tp"),
        P("rep", None, "tp"),
        P("rep", None, None),
    )
    return jax.shard_map(
        shards, mesh=mesh, in_specs=placed, out_specs=P("rep", "tp"), check_vma=False
    )
```
